1024 devices in a mesh: outer: 16 (over x, core), inner: 64 (over z, y).
Axes of the slice: x: 8, y: 8, z: 8, core: 2. Of those that a mesh axis runs over, the one named last changes fastest.
Arguments:
- code_tokens: bfloat16 [16384, 16, 768], P(('outer', 'inner')), may hold values from -24 to 24
- text_tokens: bfloat16 [16384, 16, 768], P(('outer', 'inner')), may hold values from -24 to 24
- code_weight: bfloat16 [768, 1024], replicated, may hold values from -0.21875 to 0.21875
- text_weight: bfloat16 [768, 1024], replicated, may hold values from -0.21875 to 0.21875
Outputs:
- pair_loss: float32 [16384], P(('outer', 'inner'))
- grad_code: bfloat16 [16384, 768], P(('outer', 'inner'))
- grad_text: bfloat16 [16384, 768], P(('outer', 'inner'))
The draws below stay inside these ranges and needn't reach their ends.
All inputs are finite; a program needn't handle non-finite values.
Results may differ from the reference program's by a relative error of at most 0.025.
Values may be sent and summed in bfloat16 or wider, within the bound.
No kernel may reach another device: no remote copies, remote signals or barrier semaphores. Data moves between devices by JAX's collectives and lax.ppermute only.
A program may use at most 32 MiB of HBM per device.

```python
import math
import jax
import jax.numpy as jnp
from jax import lax

D = 768
P_SIZE = 1024
SEQ = 16
PAIRS = 16384


def block_levels(rng, shape, pieces, low, top_value):
    def one(dim, shards_of):
        steps = jax.random.uniform(jax.random.fold_in(jax.random.fold_in(rng, 6), dim), (shards_of,), jnp.float32, low / len(pieces), top_value / len(pieces))
        return jnp.repeat(jnp.exp(steps), shape[dim] // shards_of).reshape((-1,) + (1,) * (len(shape) - dim - 1))

    level = one(*pieces[0])
    for cut in pieces[1:]:
        level = level * one(*cut)
    return level


def centred(rng, dims, deviation, reach, cuts=(), kind=jnp.bfloat16):
    drawn = jax.random.normal(rng, dims, jnp.float32) * deviation
    if len(cuts) > 0:
        drawn = block_levels(rng, dims, cuts, -0.22, 0.18) * drawn
    return jnp.clip(drawn, min=-reach, max=reach).astype(kind)


def setup_inputs(seed: int = 0) -> dict:
    streams_of = jax.random.split(jax.random.key(seed), 5)
    return {
        "code_tokens": centred(streams_of[0], (PAIRS, SEQ, D), 4.0, 24.0, ((0, 1024),)),
        "text_tokens": centred(streams_of[1], (PAIRS, SEQ, D), 4.0, 24.0, ((0, 1024),)),
        "code_weight": centred(streams_of[2], (D, P_SIZE), D ** -0.5, 0.21875),
        "text_weight": centred(streams_of[3], (D, P_SIZE), D ** -0.5, 0.21875),
    }


score_scale = 0.1


def reference(code_tokens, text_tokens, code_weight, text_weight):
    code_rows = jnp.mean(code_tokens.astype(jnp.float32), axis=1).astype(jnp.bfloat16)
    text_rows = jnp.mean(text_tokens.astype(jnp.float32), axis=1).astype(jnp.bfloat16)
    code_proj = jnp.dot(code_rows, code_weight, preferred_element_type=jnp.float32).astype(jnp.bfloat16)
    text_proj = jnp.dot(text_rows, text_weight, preferred_element_type=jnp.float32).astype(jnp.bfloat16)
    block = math.gcd(PAIRS, 1024)
    blocks = code_proj.reshape(PAIRS // block, block, P_SIZE)

    def first(col_acc, code_blk):
        scores = jnp.dot(code_blk, text_proj.T, preferred_element_type=jnp.float32) * score_scale
        exps = jnp.exp(scores)
        return col_acc + jnp.sum(exps, axis=0), jnp.sum(exps, axis=1)

    col_total, row_parts = lax.scan(first, jnp.zeros((PAIRS,), jnp.float32), blocks)
    row_total = row_parts.reshape(PAIRS)
    own_scores = jnp.sum(code_proj.astype(jnp.float32) * text_proj.astype(jnp.float32), axis=1) * score_scale
    pair_loss = 0.5 * (jnp.log(row_total) + jnp.log(col_total)) - own_scores

    def second(text_acc, inputs):
        code_blk, row_blk = inputs
        scores = jnp.dot(code_blk, text_proj.T, preferred_element_type=jnp.float32) * score_scale
        exps = jnp.exp(scores)
        mixing = (0.5 * (exps / row_blk[:, None] + exps / col_total[None, :])).astype(jnp.bfloat16)
        code_part = jnp.dot(mixing, text_proj, preferred_element_type=jnp.float32)
        return text_acc + jnp.dot(mixing.T, code_blk, preferred_element_type=jnp.float32), code_part

    text_sum, code_parts = lax.scan(second, jnp.zeros((PAIRS, P_SIZE), jnp.float32), (blocks, row_total.reshape(PAIRS // block, block)))
    code_sum = code_parts.reshape(PAIRS, P_SIZE)
    grad_cproj = score_scale * (code_sum - text_proj.astype(jnp.float32))
    grad_tproj = score_scale * (text_sum - code_proj.astype(jnp.float32))
    grad_code = jnp.dot(grad_cproj, code_weight.astype(jnp.float32).T, precision=lax.Precision.HIGHEST)
    grad_text = jnp.dot(grad_tproj, text_weight.astype(jnp.float32).T, precision=lax.Precision.HIGHEST)
    return pair_loss, grad_code.astype(jnp.bfloat16), grad_text.astype(jnp.bfloat16)
```

```python
import math

import jax
import jax.numpy as jnp
from jax import lax
from jax.sharding import Mesh
from jax.sharding import PartitionSpec as P

score_scale = 0.1
CODE = ("zl", "y")
TEXT = ("x", "zh")


def fan_out(block, axes):
    members = lax.axis_size(axes)
    spread = jnp.broadcast_to(block[None], (members,) + block.shape)
    spread = lax.optimization_barrier(spread)
    return lax.all_to_all(spread, axes, split_axis=0, concat_axis=0, tiled=True)


def shards(code_tokens, text_tokens, code_weight, text_weight):
    f32, bf16 = jnp.float32, jnp.bfloat16
    here, _, depth = code_tokens.shape
    core = lax.axis_index("c")
    code_row = lax.axis_index(("c",) + CODE) * here
    text_row = lax.axis_index(TEXT) * here

    code_rows = jnp.mean(code_tokens.astype(f32), axis=1).astype(bf16)
    text_rows = jnp.mean(text_tokens.astype(f32), axis=1).astype(bf16)
    code_group = fan_out(code_rows, CODE).reshape(-1, depth)
    code_group = lax.all_gather(code_group, "c", axis=0, tiled=True)
    text_group = fan_out(text_rows, TEXT).reshape(-1, depth)

    code_proj = jnp.dot(code_group, code_weight, preferred_element_type=f32).astype(bf16)
    text_proj = jnp.dot(text_group, text_weight, preferred_element_type=f32).astype(bf16)
    nt = (((1,), (1,)), ((), ()))
    scores = lax.dot_general(code_proj, text_proj, nt, preferred_element_type=f32) * score_scale
    exps = jnp.exp(scores)
    row_part = jnp.sum(exps, axis=1)
    col_part = jnp.sum(exps, axis=0)
    row_part = jnp.sum(lax.all_gather(row_part, "c", axis=0), axis=0)
    row_total = jnp.sum(fan_out(row_part, CODE), axis=0)
    col_total = jnp.sum(fan_out(col_part, TEXT), axis=0)

    own = jnp.eye(here, dtype=f32)
    own_scores = jnp.sum(lax.dynamic_slice(scores, (code_row, text_row), (here, here)) * own, axis=1)
    own_row_total = lax.dynamic_slice_in_dim(row_total, code_row, here)
    own_col_total = lax.dynamic_slice_in_dim(col_total, text_row, here)
    pair_loss = 0.5 * (jnp.log(own_row_total) + jnp.log(own_col_total)) - own_scores

    rows = lax.broadcasted_iota(jnp.int32, scores.shape, 0) - code_row
    cols = lax.broadcasted_iota(jnp.int32, scores.shape, 1) - text_row
    paired = (rows == cols) & (rows >= 0) & (rows < here)
    mixing = 0.5 * (exps / row_total[:, None] + exps / col_total[None, :])
    mixing = (mixing - jnp.where(paired, 1.0, 0.0)).astype(bf16)

    text_back = lax.dot_general(text_proj, code_weight, nt, preferred_element_type=f32).astype(bf16)
    code_back = lax.dot_general(code_proj, text_weight, nt, preferred_element_type=f32).astype(bf16)
    code_term = jnp.dot(mixing, text_back, preferred_element_type=f32)
    text_term = lax.dot_general(
        mixing, code_back, (((0,), (0,)), ((), ())), preferred_element_type=f32
    )

    code_term = code_term.reshape(2, -1, here, depth)
    theirs = lax.dynamic_index_in_dim(code_term, 1 - core, 0, keepdims=False).astype(bf16)
    mine = lax.dynamic_index_in_dim(code_term, core, 0, keepdims=False)
    theirs = lax.ppermute(theirs, "c", [(0, 1), (1, 0)])
    code_parts = (mine + theirs.astype(f32)).astype(bf16)
    code_parts = lax.all_to_all(code_parts, CODE, split_axis=0, concat_axis=0, tiled=True)
    text_parts = text_term.reshape(-1, here, depth).astype(bf16)
    text_parts = lax.all_to_all(text_parts, TEXT, split_axis=0, concat_axis=0, tiled=True)
    grad_code = score_scale * jnp.sum(code_parts.astype(f32), axis=0)
    grad_text = score_scale * jnp.sum(text_parts.astype(f32), axis=0)
    return pair_loss, grad_code.astype(bf16), grad_text.astype(bf16)


def solution(mesh):
    n_outer, n_inner = mesh.shape["outer"], mesh.shape["inner"]
    side = math.isqrt(n_inner)
    fine = Mesh(
        mesh.devices.reshape(n_outer // 2, 2, side // 2, 2, side), ("x", "c", "zh", "zl", "y")
    )
    every = P(fine.axis_names)
    return jax.shard_map(
        shards,
        mesh=fine,
        in_specs=(every, every, P(), P()),
        out_specs=(every, every, every),
        check_vma=False,
    )
```

```python
import math

import jax
import jax.numpy as jnp
from jax import lax
from jax.sharding import Mesh
from jax.sharding import PartitionSpec as P

score_scale = 0.1
CODE = ("y", "c", "zl")
TEXT = ("x", "zh")


def fan_out(block, axes):
    members = lax.axis_size(axes)
    spread = jnp.broadcast_to(block[None], (members,) + block.shape)
    spread = lax.optimization_barrier(spread)
    return lax.all_to_all(spread, axes, split_axis=0, concat_axis=0, tiled=True)


def gather_code(block):
    pair = lax.all_gather(block, "zl", axis=0, tiled=True)
    return lax.all_gather(pair, ("y", "c"), axis=0, tiled=True)


def add_half(parts, axis, name):
    me = lax.axis_index(name)
    mine = lax.dynamic_index_in_dim(parts, me, axis, keepdims=False)
    theirs = lax.dynamic_index_in_dim(parts, 1 - me, axis, keepdims=False).astype(jnp.bfloat16)
    theirs = lax.ppermute(theirs, name, [(0, 1), (1, 0)])
    return mine.astype(jnp.float32) + theirs.astype(jnp.float32)


def shards(code_tokens, text_tokens, code_weight, text_weight):
    f32, bf16 = jnp.float32, jnp.bfloat16
    here, _, depth = code_tokens.shape
    code_row = lax.axis_index(CODE) * here
    text_row = lax.axis_index(TEXT) * here

    text_rows = jnp.mean(text_tokens.astype(f32), axis=1).astype(bf16)
    text_group = fan_out(text_rows, TEXT).reshape(-1, depth)
    code_rows = jnp.mean(code_tokens.astype(f32), axis=1).astype(bf16)
    code_group = gather_code(code_rows)

    code_proj = jnp.dot(code_group, code_weight, preferred_element_type=f32).astype(bf16)
    text_proj = jnp.dot(text_group, text_weight, preferred_element_type=f32).astype(bf16)
    nt = (((1,), (1,)), ((), ()))
    scores = lax.dot_general(code_proj, text_proj, nt, preferred_element_type=f32) * score_scale
    exps = jnp.exp(scores)
    row_part = jnp.sum(exps, axis=1)
    col_part = jnp.sum(exps, axis=0)
    col_total = jnp.sum(fan_out(col_part, TEXT), axis=0)
    row_total = jnp.sum(gather_code(row_part[None]), axis=0)
    text_back = lax.dot_general(text_proj, code_weight, nt, preferred_element_type=f32).astype(bf16)
    code_back = lax.dot_general(code_proj, text_weight, nt, preferred_element_type=f32).astype(bf16)
    text_back, code_back = lax.optimization_barrier((text_back, code_back))

    own = jnp.eye(here, dtype=f32)
    own_scores = jnp.sum(lax.dynamic_slice(scores, (code_row, text_row), (here, here)) * own, axis=1)
    own_row_total = lax.dynamic_slice_in_dim(row_total, code_row, here)
    own_col_total = lax.dynamic_slice_in_dim(col_total, text_row, here)
    pair_loss = 0.5 * (jnp.log(own_row_total) + jnp.log(own_col_total)) - own_scores

    rows = lax.broadcasted_iota(jnp.int32, scores.shape, 0) - code_row
    cols = lax.broadcasted_iota(jnp.int32, scores.shape, 1) - text_row
    paired = (rows == cols) & (rows >= 0) & (rows < here)
    mixing = 0.5 * (exps / row_total[:, None] + exps / col_total[None, :])
    mixing = (mixing - jnp.where(paired, 1.0, 0.0)).astype(bf16)

    text_term = lax.dot_general(
        mixing, code_back, (((0,), (0,)), ((), ())), preferred_element_type=f32
    )
    text_parts = text_term.reshape(-1, here, depth).astype(bf16)
    mixing, text_parts = lax.optimization_barrier((mixing, text_parts))
    text_parts = lax.all_to_all(text_parts, TEXT, split_axis=0, concat_axis=0, tiled=True)
    code_term = jnp.dot(mixing, text_back, preferred_element_type=f32)
    code_parts = code_term.reshape(-1, 2, 2, here, depth)
    code_parts = add_half(code_parts, 1, "c")
    code_parts = add_half(code_parts, 1, "zl").astype(bf16)
    code_parts, text_parts = lax.optimization_barrier((code_parts, text_parts))
    code_parts = lax.all_to_all(code_parts, "y", split_axis=0, concat_axis=0, tiled=True)
    grad_code = score_scale * jnp.sum(code_parts.astype(f32), axis=0)
    grad_text = score_scale * jnp.sum(text_parts.astype(f32), axis=0)
    return pair_loss, grad_code.astype(bf16), grad_text.astype(bf16)


def solution(mesh):
    n_outer, n_inner = mesh.shape["outer"], mesh.shape["inner"]
    side = math.isqrt(n_inner)
    fine = Mesh(
        mesh.devices.reshape(n_outer // 2, 2, side // 2, 2, side), ("x", "c", "zh", "zl", "y")
    )
    every = P(fine.axis_names)
    return jax.shard_map(
        shards,
        mesh=fine,
        in_specs=(every, every, P(), P()),
        out_specs=(every, every, every),
        check_vma=False,
    )
```

```python
import math

import jax
import jax.numpy as jnp
from jax import lax
from jax.sharding import Mesh
from jax.sharding import PartitionSpec as P

score_scale = 0.1
CODE = ("y", "c", "zl")
TEXT = ("x", "zh")


def fan_out(block, axes):
    members = lax.axis_size(axes)
    spread = jnp.broadcast_to(block[None], (members,) + block.shape)
    spread = lax.optimization_barrier(spread)
    return lax.all_to_all(spread, axes, split_axis=0, concat_axis=0, tiled=True)


def gather_code(block):
    pair = lax.all_gather(block, "zl", axis=0, tiled=True)
    return lax.all_gather(pair, ("y", "c"), axis=0, tiled=True)


def add_half(parts, axis, name):
    me = lax.axis_index(name)
    mine = lax.dynamic_index_in_dim(parts, me, axis, keepdims=False)
    theirs = lax.dynamic_index_in_dim(parts, 1 - me, axis, keepdims=False).astype(jnp.bfloat16)
    theirs = lax.ppermute(theirs, name, [(0, 1), (1, 0)])
    return mine.astype(jnp.float32) + theirs.astype(jnp.float32)


def shards(code_tokens, text_tokens, code_weight, text_weight):
    f32, bf16 = jnp.float32, jnp.bfloat16
    here, _, depth = code_tokens.shape
    code_row = lax.axis_index(CODE) * here
    text_row = lax.axis_index(TEXT) * here

    code_rows = jnp.mean(code_tokens.astype(f32), axis=1).astype(bf16)
    text_rows = jnp.mean(text_tokens.astype(f32), axis=1).astype(bf16)
    code_pair = lax.all_gather(code_rows, "zl", axis=0, tiled=True)
    code_pair, text_rows = lax.optimization_barrier((code_pair, text_rows))
    text_group = fan_out(text_rows, TEXT).reshape(-1, depth)
    code_group = lax.all_gather(code_pair, ("y", "c"), axis=0, tiled=True)

    nt = (((1,), (1,)), ((), ()))
    code_proj = jnp.dot(code_group, code_weight, preferred_element_type=f32).astype(bf16)
    code_back = lax.dot_general(code_proj, text_weight, nt, preferred_element_type=f32).astype(bf16)
    code_back = lax.optimization_barrier(code_back)
    text_proj = jnp.dot(text_group, text_weight, preferred_element_type=f32).astype(bf16)
    scores = lax.dot_general(code_proj, text_proj, nt, preferred_element_type=f32) * score_scale
    exps = jnp.exp(scores)
    row_part = jnp.sum(exps, axis=1)
    col_part = jnp.sum(exps, axis=0)
    col_total = jnp.sum(fan_out(col_part, TEXT), axis=0)
    row_total = jnp.sum(gather_code(row_part[None]), axis=0)
    own = jnp.eye(here, dtype=f32)
    own_scores = jnp.sum(lax.dynamic_slice(scores, (code_row, text_row), (here, here)) * own, axis=1)
    own_row_total = lax.dynamic_slice_in_dim(row_total, code_row, here)
    own_col_total = lax.dynamic_slice_in_dim(col_total, text_row, here)
    pair_loss = 0.5 * (jnp.log(own_row_total) + jnp.log(own_col_total)) - own_scores

    rows = lax.broadcasted_iota(jnp.int32, scores.shape, 0) - code_row
    cols = lax.broadcasted_iota(jnp.int32, scores.shape, 1) - text_row
    paired = (rows == cols) & (rows >= 0) & (rows < here)
    mixing = 0.5 * (exps / row_total[:, None] + exps / col_total[None, :])
    mixing = (mixing - jnp.where(paired, 1.0, 0.0)).astype(bf16)

    text_term = lax.dot_general(
        mixing, code_back, (((0,), (0,)), ((), ())), preferred_element_type=f32
    )
    text_parts = text_term.reshape(-1, here, depth).astype(bf16)
    mixing, text_proj, text_parts = lax.optimization_barrier((mixing, text_proj, text_parts))
    text_parts = lax.all_to_all(text_parts, TEXT, split_axis=0, concat_axis=0, tiled=True)
    text_back = lax.dot_general(text_proj, code_weight, nt, preferred_element_type=f32).astype(bf16)
    code_term = jnp.dot(mixing, text_back, preferred_element_type=f32)
    code_parts = add_half(code_term.reshape(-1, 2, 2 * here, depth), 1, "c")
    code_parts = code_parts.reshape(-1, here, depth).astype(bf16)
    code_parts, text_parts = lax.optimization_barrier((code_parts, text_parts))
    code_parts = lax.all_to_all(code_parts, ("y", "zl"), split_axis=0, concat_axis=0, tiled=True)
    grad_code = score_scale * jnp.sum(code_parts.astype(f32), axis=0)
    grad_text = score_scale * jnp.sum(text_parts.astype(f32), axis=0)
    return pair_loss, grad_code.astype(bf16), grad_text.astype(bf16)


def solution(mesh):
    n_outer, n_inner = mesh.shape["outer"], mesh.shape["inner"]
    side = math.isqrt(n_inner)
    fine = Mesh(
        mesh.devices.reshape(n_outer // 2, 2, side // 2, 2, side), ("x", "c", "zh", "zl", "y")
    )
    every = P(fine.axis_names)
    return jax.shard_map(
        shards,
        mesh=fine,
        in_specs=(every, every, P(), P()),
        out_specs=(every, every, every),
        check_vma=False,
    )
```

```python
import math

import jax
import jax.numpy as jnp
from jax import lax
from jax.sharding import Mesh
from jax.sharding import PartitionSpec as P

score_scale = 0.1
CODE = ("yh", "yl", "c", "zl")
TEXT = ("xl", "xh", "zh")


def fan_out(block, axes):
    members = lax.axis_size(axes)
    spread = jnp.broadcast_to(block[None], (members,) + block.shape)
    spread = lax.optimization_barrier(spread)
    return lax.all_to_all(spread, axes, split_axis=0, concat_axis=0, tiled=True)


def add_half(term, name):
    me = lax.axis_index(name)
    theirs = lax.ppermute(term(1 - me).astype(jnp.bfloat16), name, [(0, 1), (1, 0)])
    return (term(me).astype(jnp.float32) + theirs.astype(jnp.float32)).astype(jnp.bfloat16)


def shards(code_tokens, text_tokens, code_weight, text_weight):
    f32, bf16 = jnp.float32, jnp.bfloat16
    nt = (((1,), (1,)), ((), ()))
    here, _, depth = code_tokens.shape
    code_row = lax.axis_index(CODE) * here
    text_row = lax.axis_index(TEXT) * here

    code_rows = jnp.mean(code_tokens.astype(f32), axis=1).astype(bf16)
    text_rows = jnp.mean(text_tokens.astype(f32), axis=1).astype(bf16)
    code_pair = lax.all_gather(code_rows, "zl", axis=0, tiled=True)
    code_pair, text_rows = lax.optimization_barrier((code_pair, text_rows))
    text_group = fan_out(text_rows, TEXT).reshape(-1, depth)
    code_group = lax.all_gather(code_pair, CODE[:3], axis=0, tiled=True)

    code_proj = jnp.dot(code_group, code_weight, preferred_element_type=f32).astype(bf16)
    text_proj = jnp.dot(text_group, text_weight, preferred_element_type=f32).astype(bf16)
    scores = lax.dot_general(code_proj, text_proj, nt, preferred_element_type=f32) * score_scale
    exps = jnp.exp(scores)
    row_part = jnp.sum(exps, axis=1)
    col_part = jnp.sum(exps, axis=0)
    col_parts = fan_out(col_part, TEXT)
    row_part = jnp.sum(lax.all_gather(row_part, ("zl", "c"), axis=0), axis=0)
    row_part, col_parts, code_proj, text_proj = lax.optimization_barrier(
        (row_part, col_parts, code_proj, text_proj)
    )
    col_total = jnp.sum(col_parts, axis=0)
    row_total = jnp.sum(fan_out(row_part, CODE[:2]), axis=0)
    text_back = lax.dot_general(text_proj, code_weight, nt, preferred_element_type=f32).astype(bf16)
    code_back = lax.dot_general(code_proj, text_weight, nt, preferred_element_type=f32).astype(bf16)
    text_back, code_back = lax.optimization_barrier((text_back, code_back))

    own = jnp.eye(here, dtype=f32)
    own_scores = jnp.sum(lax.dynamic_slice(scores, (code_row, text_row), (here, here)) * own, axis=1)
    own_row_total = lax.dynamic_slice_in_dim(row_total, code_row, here)
    own_col_total = lax.dynamic_slice_in_dim(col_total, text_row, here)
    pair_loss = 0.5 * (jnp.log(own_row_total) + jnp.log(own_col_total)) - own_scores

    rows = lax.broadcasted_iota(jnp.int32, scores.shape, 0) - code_row
    cols = lax.broadcasted_iota(jnp.int32, scores.shape, 1) - text_row
    paired = (rows == cols) & (rows >= 0) & (rows < here)
    mixing = 0.5 * (exps / row_total[:, None] + exps / col_total[None, :])
    mixing = (mixing - jnp.where(paired, 1.0, 0.0)).astype(bf16)

    def text_half(half):
        part = lax.dynamic_index_in_dim(mixing.reshape(-1, 2, cols_half), half, 1, keepdims=False)
        return lax.dot_general(part, code_back, (((0,), (0,)), ((), ())), preferred_element_type=f32)

    def code_half(half):
        part = lax.dynamic_index_in_dim(by_core, half, 1, keepdims=False)
        return jnp.dot(part.reshape(-1, part.shape[-1]), text_back, preferred_element_type=f32)

    cols_half = mixing.shape[1] // 2
    by_core = mixing.reshape(-1, 2, 2 * here, mixing.shape[1])
    text_parts = add_half(text_half, "xl").reshape(-1, here, depth)
    text_parts = lax.all_to_all(text_parts, TEXT[1:], split_axis=0, concat_axis=0, tiled=True)
    by_row = add_half(code_half, "c").reshape(-1, 2, 2 * here, depth)
    code_parts = add_half(lambda i: lax.dynamic_index_in_dim(by_row, i, 1, keepdims=False), "yl")
    code_parts, text_parts = lax.optimization_barrier((code_parts, text_parts))
    code_parts = code_parts.reshape(-1, here, depth)
    code_parts = lax.all_to_all(code_parts, ("yh", "zl"), split_axis=0, concat_axis=0, tiled=True)
    grad_code = score_scale * jnp.sum(code_parts.astype(f32), axis=0)
    grad_text = score_scale * jnp.sum(text_parts.astype(f32), axis=0)
    return pair_loss, grad_code.astype(bf16), grad_text.astype(bf16)


def solution(mesh):
    n_outer, n_inner = mesh.shape["outer"], mesh.shape["inner"]
    side = math.isqrt(n_inner)
    sizes = (n_outer // 4, 2, 2, side // 2, 2, side // 2, 2)
    fine = Mesh(mesh.devices.reshape(sizes), ("xh", "xl", "c", "zh", "zl", "yh", "yl"))
    every = P(fine.axis_names)
    return jax.shard_map(
        shards,
        mesh=fine,
        in_specs=(every, every, P(), P()),
        out_specs=(every, every, every),
        check_vma=False,
    )
```

```python
import math

import jax
import jax.numpy as jnp
from jax import lax
from jax.experimental import pallas as pl
from jax.experimental.pallas import tpu as pltpu
from jax.sharding import Mesh
from jax.sharding import PartitionSpec as P

score_scale = 0.1
CODE = ("yh", "yl", "c", "zl")
TEXT = ("x", "zh")


def pool_kernel(code_ref, text_ref, code_out, text_out):
    for tokens, out in ((code_ref, code_out), (text_ref, text_out)):
        total = jnp.sum(tokens[...].astype(jnp.float32), axis=1)
        rows = (total * (1.0 / tokens.shape[1])).astype(jnp.bfloat16)
        out[...] = rows if out is code_out else jnp.broadcast_to(rows[None], out.shape)


def pool(code_tokens, text_tokens, copies):
    here, _, depth = code_tokens.shape
    return pl.pallas_call(
        pool_kernel,
        out_shape=(
            jax.ShapeDtypeStruct((here, depth), jnp.bfloat16),
            jax.ShapeDtypeStruct((copies, here, depth), jnp.bfloat16),
        ),
    )(code_tokens, text_tokens)


def exchange(parts, axes):
    return lax.all_to_all(parts, axes, split_axis=0, concat_axis=0, tiled=True)


def fan_out(block, axes):
    members = lax.axis_size(axes)
    spread = jnp.broadcast_to(block[None], (members,) + block.shape)
    return exchange(lax.optimization_barrier(spread), axes)


def swap(block, name):
    return lax.ppermute(block, name, [(0, 1), (1, 0)])


def code_sum_kernel(core_ref, mixing_ref, text_ref, weight_ref, mine_ref, theirs_ref, back_ref, rows_ref):
    nt = (((1,), (1,)), ((), ()))
    step = text_ref.shape[0] // 2
    for i in range(2):
        part = text_ref[i * step : (i + 1) * step, :]
        back = lax.dot_general(part, weight_ref[...], nt, preferred_element_type=jnp.float32)
        back_ref[i * step : (i + 1) * step, :] = back.astype(jnp.bfloat16)
    chunk = 32
    for core, out_ref in ((1 - core_ref[0], theirs_ref), (core_ref[0], mine_ref)):
        for i in range(out_ref.shape[0] // chunk):
            start = pl.multiple_of(core * chunk + 2 * i * chunk, chunk)
            rows_ref[i * chunk : (i + 1) * chunk, :] = mixing_ref[pl.ds(start, chunk), :]
        total = jnp.dot(rows_ref[...], back_ref[...], preferred_element_type=jnp.float32)
        out_ref[...] = total.astype(out_ref.dtype)


def code_sum(core, mixing, text_proj, weight):
    rows, cols = mixing.shape
    depth = weight.shape[0]
    vmem = pl.BlockSpec(memory_space=pltpu.VMEM)
    half = jax.ShapeDtypeStruct((rows // 2, depth), jnp.bfloat16)
    return pl.pallas_call(
        code_sum_kernel,
        out_shape=(half, half),
        in_specs=[pl.BlockSpec(memory_space=pltpu.SMEM), vmem, vmem, vmem],
        out_specs=(vmem, vmem),
        scratch_shapes=[
            pltpu.VMEM((cols, depth), jnp.bfloat16),
            pltpu.VMEM((rows // 2, cols), jnp.bfloat16),
        ],
        compiler_params=pltpu.CompilerParams(vmem_limit_bytes=32 << 20),
        cost_estimate=pl.CostEstimate(flops=1 << 28, bytes_accessed=1 << 20, transcendentals=0),
    )(core.reshape(1), mixing, text_proj, weight)


def shards(code_tokens, text_tokens, code_weight, text_weight):
    f32, bf16 = jnp.float32, jnp.bfloat16
    nt = (((1,), (1,)), ((), ()))
    here, _, depth = code_tokens.shape
    code_row = lax.axis_index(CODE) * here
    text_row = lax.axis_index(TEXT) * here

    code_rows, text_rows = pool(code_tokens, text_tokens, lax.axis_size(TEXT))
    code_pair = lax.all_gather(code_rows, "zl", axis=0, tiled=True)
    code_pair, text_rows = lax.optimization_barrier((code_pair, text_rows))
    text_group = exchange(text_rows, TEXT).reshape(-1, depth)
    code_group = lax.all_gather(code_pair, CODE[:3], axis=0, tiled=True)

    code_proj = jnp.dot(code_group, code_weight, preferred_element_type=f32).astype(bf16)
    code_back = lax.dot_general(code_proj, text_weight, nt, preferred_element_type=f32).astype(bf16)
    code_back, text_group = lax.optimization_barrier((code_back, text_group))
    text_proj = jnp.dot(text_group, text_weight, preferred_element_type=f32).astype(bf16)
    scores = lax.dot_general(code_proj, text_proj, nt, preferred_element_type=f32) * score_scale
    exps = jnp.exp(scores)
    row_part = jnp.sum(exps, axis=1)
    col_part = jnp.sum(exps, axis=0)
    row_part = row_part + swap(row_part, "zl")
    col_total = jnp.sum(fan_out(col_part, TEXT), axis=0)
    row_total = jnp.sum(lax.all_gather(row_part, CODE[:3], axis=0), axis=0)

    own = jnp.eye(here, dtype=f32)
    own_scores = jnp.sum(lax.dynamic_slice(scores, (code_row, text_row), (here, here)) * own, axis=1)
    own_row_total = lax.dynamic_slice_in_dim(row_total, code_row, here)
    own_col_total = lax.dynamic_slice_in_dim(col_total, text_row, here)
    pair_loss = 0.5 * (jnp.log(own_row_total) + jnp.log(own_col_total)) - own_scores

    rows = lax.broadcasted_iota(jnp.int32, scores.shape, 0) - code_row
    cols = lax.broadcasted_iota(jnp.int32, scores.shape, 1) - text_row
    paired = (rows == cols) & (rows >= 0) & (rows < here)
    mixing = 0.5 * (exps / row_total[:, None] + exps / col_total[None, :])
    mixing = (mixing - jnp.where(paired, 1.0, 0.0)).astype(bf16)

    text_term = lax.dot_general(
        mixing, code_back, (((0,), (0,)), ((), ())), preferred_element_type=f32
    )
    text_proj, text_parts = lax.optimization_barrier((text_proj, text_term.astype(bf16)))
    text_parts = exchange(text_parts.reshape(-1, here, depth), TEXT)

    mine, theirs = code_sum(lax.axis_index("c"), mixing, text_proj, code_weight)
    code_parts = (mine.astype(f32) + swap(theirs, "c").astype(f32)).astype(bf16)
    code_parts = code_parts.reshape(-1, 2, 2 * here, depth)
    side = lax.axis_index("yl")
    mine = lax.dynamic_index_in_dim(code_parts, side, 1, keepdims=False)
    theirs = lax.dynamic_index_in_dim(code_parts, 1 - side, 1, keepdims=False)
    code_parts = (mine.astype(f32) + swap(theirs, "yl").astype(f32)).astype(bf16)
    code_parts, text_parts = lax.optimization_barrier((code_parts, text_parts))
    code_parts = exchange(code_parts.reshape(-1, here, depth), ("yh", "zl"))
    grad_code = score_scale * jnp.sum(code_parts.astype(f32), axis=0)
    grad_text = score_scale * jnp.sum(text_parts.astype(f32), axis=0)
    return pair_loss, grad_code.astype(bf16), grad_text.astype(bf16)


def solution(mesh):
    n_outer, n_inner = mesh.shape["outer"], mesh.shape["inner"]
    side = math.isqrt(n_inner)
    sizes = (n_outer // 2, 2, side // 2, 2, side // 2, 2)
    fine = Mesh(mesh.devices.reshape(sizes), ("x", "c", "zh", "zl", "yh", "yl"))
    every = P(fine.axis_names)
    return jax.shard_map(
        shards,
        mesh=fine,
        in_specs=(every, every, P(), P()),
        out_specs=(every, every, every),
        check_vma=False,
    )
```

```python
import math

import jax
import jax.numpy as jnp
from jax import lax
from jax.experimental import pallas as pl
from jax.experimental.pallas import tpu as pltpu
from jax.sharding import Mesh
from jax.sharding import PartitionSpec as P

score_scale = 0.1
CODE = ("yh", "yl", "c", "zl")
ROWS = ("c", "zl", "yh", "yl")
TEXT = ("x", "zh")


def pool_kernel(code_ref, text_ref, code_out, text_out):
    for tokens, out in ((code_ref, code_out), (text_ref, text_out)):
        total = jnp.sum(tokens[...].astype(jnp.float32), axis=1)
        rows = (total * (1.0 / tokens.shape[1])).astype(jnp.bfloat16)
        out[...] = rows if out is code_out else jnp.broadcast_to(rows[None], out.shape)


def pool(code_tokens, text_tokens, copies):
    here, _, depth = code_tokens.shape
    return pl.pallas_call(
        pool_kernel,
        out_shape=(
            jax.ShapeDtypeStruct((here, depth), jnp.bfloat16),
            jax.ShapeDtypeStruct((copies, here, depth), jnp.bfloat16),
        ),
    )(code_tokens, text_tokens)


def exchange(parts, axes):
    return lax.all_to_all(parts, axes, split_axis=0, concat_axis=0, tiled=True)


def fan_out(block, axes):
    members = lax.axis_size(axes)
    spread = jnp.broadcast_to(block[None], (members,) + block.shape)
    return exchange(lax.optimization_barrier(spread), axes)


def swap(block, name):
    return lax.ppermute(block, name, [(0, 1), (1, 0)])


def code_sum_kernel(core_ref, mixing_ref, text_ref, weight_ref, mine_ref, theirs_ref, back_ref, rows_ref):
    nt = (((1,), (1,)), ((), ()))
    step = text_ref.shape[0] // 2
    for i in range(2):
        part = text_ref[i * step : (i + 1) * step, :]
        back = lax.dot_general(part, weight_ref[...], nt, preferred_element_type=jnp.float32)
        back_ref[i * step : (i + 1) * step, :] = back.astype(jnp.bfloat16)
    chunk = 32
    for core, out_ref in ((1 - core_ref[0], theirs_ref), (core_ref[0], mine_ref)):
        for i in range(out_ref.shape[0] // chunk):
            start = pl.multiple_of(core * chunk + 2 * i * chunk, chunk)
            rows_ref[i * chunk : (i + 1) * chunk, :] = mixing_ref[pl.ds(start, chunk), :]
        total = jnp.dot(rows_ref[...], back_ref[...], preferred_element_type=jnp.float32)
        out_ref[...] = total.astype(out_ref.dtype)


def code_sum(core, mixing, text_proj, weight):
    rows, cols = mixing.shape
    depth = weight.shape[0]
    vmem = pl.BlockSpec(memory_space=pltpu.VMEM)
    half = jax.ShapeDtypeStruct((rows // 2, depth), jnp.bfloat16)
    return pl.pallas_call(
        code_sum_kernel,
        out_shape=(half, half),
        in_specs=[pl.BlockSpec(memory_space=pltpu.SMEM), vmem, vmem, vmem],
        out_specs=(vmem, vmem),
        scratch_shapes=[
            pltpu.VMEM((cols, depth), jnp.bfloat16),
            pltpu.VMEM((rows // 2, cols), jnp.bfloat16),
        ],
        compiler_params=pltpu.CompilerParams(vmem_limit_bytes=32 << 20),
        cost_estimate=pl.CostEstimate(flops=1 << 28, bytes_accessed=1 << 20, transcendentals=0),
    )(core.reshape(1), mixing, text_proj, weight)


def shards(code_tokens, text_tokens, code_weight, text_weight):
    f32, bf16 = jnp.float32, jnp.bfloat16
    nt = (((1,), (1,)), ((), ()))
    here, _, depth = code_tokens.shape
    core, side = lax.axis_index("c"), lax.axis_index("yl")
    code_row = lax.axis_index(CODE) * here
    text_row = lax.axis_index(TEXT) * here

    code_rows, text_rows = pool(code_tokens, text_tokens, lax.axis_size(TEXT))
    code_pair = lax.all_gather(code_rows, "zl", axis=0, tiled=True)
    code_pair, text_rows = lax.optimization_barrier((code_pair, text_rows))
    text_group = exchange(text_rows, TEXT).reshape(-1, depth)
    code_group = lax.all_gather(code_pair, CODE[:3], axis=0, tiled=True)

    code_proj = jnp.dot(code_group, code_weight, preferred_element_type=f32).astype(bf16)
    code_back = lax.dot_general(code_proj, text_weight, nt, preferred_element_type=f32).astype(bf16)
    code_back, text_group = lax.optimization_barrier((code_back, text_group))
    text_proj = jnp.dot(text_group, text_weight, preferred_element_type=f32).astype(bf16)
    scores = lax.dot_general(code_proj, text_proj, nt, preferred_element_type=f32) * score_scale
    exps = jnp.exp(scores)
    row_part = jnp.sum(exps, axis=1)
    col_part = jnp.sum(exps, axis=0)
    lanes = math.gcd(col_part.size, 128)
    live = (scores, exps, code_back, text_proj, code_row, text_row, core, side)
    row_part, col_part, *live = lax.optimization_barrier((row_part, col_part, *live))
    row_parts, col_part, *live = lax.optimization_barrier((fan_out(row_part.reshape(-1, lanes), ROWS), col_part, *live))
    row_parts, col_parts, *live = lax.optimization_barrier((row_parts, fan_out(col_part.reshape(-1, lanes), TEXT), *live))
    scores, exps, code_back, text_proj, code_row, text_row, core, side = live
    row_total = jnp.sum(row_parts, axis=0).reshape(-1)
    col_total = jnp.sum(col_parts, axis=0).reshape(-1)

    own = jnp.eye(here, dtype=f32)
    own_scores = jnp.sum(lax.dynamic_slice(scores, (code_row, text_row), (here, here)) * own, axis=1)
    own_row_total = lax.dynamic_slice_in_dim(row_total, code_row, here)
    own_col_total = lax.dynamic_slice_in_dim(col_total, text_row, here)
    pair_loss = 0.5 * (jnp.log(own_row_total) + jnp.log(own_col_total)) - own_scores

    rows = lax.broadcasted_iota(jnp.int32, scores.shape, 0) - code_row
    cols = lax.broadcasted_iota(jnp.int32, scores.shape, 1) - text_row
    paired = (rows == cols) & (rows >= 0) & (rows < here)
    mixing = 0.5 * (exps / row_total[:, None] + exps / col_total[None, :])
    mixing = (mixing - jnp.where(paired, 1.0, 0.0)).astype(bf16)

    text_term = lax.dot_general(
        mixing, code_back, (((0,), (0,)), ((), ())), preferred_element_type=f32
    )
    text_proj, text_parts = lax.optimization_barrier((text_proj, text_term.astype(bf16)))
    text_parts = exchange(text_parts.reshape(-1, here, depth), TEXT)

    mine, theirs = code_sum(core, mixing, text_proj, code_weight)
    code_parts = (mine.astype(f32) + swap(theirs, "c").astype(f32)).astype(bf16)
    code_parts = code_parts.reshape(-1, 2, 2 * here, depth)
    mine = lax.dynamic_index_in_dim(code_parts, side, 1, keepdims=False)
    theirs = lax.dynamic_index_in_dim(code_parts, 1 - side, 1, keepdims=False)
    code_parts = (mine.astype(f32) + swap(theirs, "yl").astype(f32)).astype(bf16)
    code_parts, text_parts = lax.optimization_barrier((code_parts, text_parts))
    code_parts = exchange(code_parts.reshape(-1, here, depth), ("yh", "zl"))
    grad_code = score_scale * jnp.sum(code_parts.astype(f32), axis=0)
    grad_text = score_scale * jnp.sum(text_parts.astype(f32), axis=0)
    return pair_loss, grad_code.astype(bf16), grad_text.astype(bf16)


def solution(mesh):
    n_outer, n_inner = mesh.shape["outer"], mesh.shape["inner"]
    side = math.isqrt(n_inner)
    sizes = (n_outer // 2, 2, side // 2, 2, side // 2, 2)
    fine = Mesh(mesh.devices.reshape(sizes), ("x", "c", "zh", "zl", "yh", "yl"))
    every = P(fine.axis_names)
    return jax.shard_map(
        shards,
        mesh=fine,
        in_specs=(every, every, P(), P()),
        out_specs=(every, every, every),
        check_vma=False,
    )
```

```python
import math

import jax
import jax.numpy as jnp
from jax import lax
from jax.experimental import pallas as pl
from jax.experimental.pallas import tpu as pltpu
from jax.sharding import Mesh
from jax.sharding import PartitionSpec as P

score_scale = 0.1
CODE = ("yh", "yl", "c", "zl")
ROWS = ("c", "zl", "yh", "yl")
TEXT = ("x", "zh")


def pool_kernel(code_ref, text_ref, code_out, text_out):
    for tokens, out in ((code_ref, code_out), (text_ref, text_out)):
        total = jnp.sum(tokens[...].astype(jnp.float32), axis=1)
        rows = (total * (1.0 / tokens.shape[1])).astype(jnp.bfloat16)
        out[...] = rows if out is code_out else jnp.broadcast_to(rows[None], out.shape)


def pool(code_tokens, text_tokens, copies):
    here, _, depth = code_tokens.shape
    return pl.pallas_call(
        pool_kernel,
        out_shape=(
            jax.ShapeDtypeStruct((here, depth), jnp.bfloat16),
            jax.ShapeDtypeStruct((copies, here, depth), jnp.bfloat16),
        ),
    )(code_tokens, text_tokens)


def exchange(parts, axes):
    return lax.all_to_all(parts, axes, split_axis=0, concat_axis=0, tiled=True)


def fan_out(block, axes):
    members = lax.axis_size(axes)
    spread = jnp.broadcast_to(block[None], (members,) + block.shape)
    return exchange(lax.optimization_barrier(spread), axes)


def score_kernel(text_ref, weight_ref, code_ref, proj_ref, exps_ref, row_ref, col_ref):
    nt = (((1,), (1,)), ((), ()))
    lanes = row_ref.shape[2]
    step = text_ref.shape[0] // 2
    row_sum = jnp.zeros((code_ref.shape[0], lanes), jnp.float32)
    for i in range(2):
        part = jnp.dot(
            text_ref[i * step : (i + 1) * step, :], weight_ref[...], preferred_element_type=jnp.float32
        ).astype(jnp.bfloat16)
        proj_ref[i * step : (i + 1) * step, :] = part
        scores = lax.dot_general(code_ref[...], part, nt, preferred_element_type=jnp.float32)
        exps = jnp.exp(scores * score_scale)
        exps_ref[:, i * step : (i + 1) * step] = exps
        col_sum = jnp.sum(exps, axis=0, keepdims=True)
        for j in range(step // lanes):
            row_sum += exps[:, j * lanes : (j + 1) * lanes]
            at = i * (step // lanes) + j
            total = jnp.broadcast_to(col_sum[:, j * lanes : (j + 1) * lanes], (col_ref.shape[0], lanes))
            col_ref[:, at, :] = total
    row_sum = jnp.sum(row_sum.T, axis=0, keepdims=True)
    for j in range(row_ref.shape[1]):
        total = jnp.broadcast_to(row_sum[:, j * lanes : (j + 1) * lanes], (row_ref.shape[0], lanes))
        row_ref[:, j, :] = total


def score_blocks(text_group, weight, code_proj, row_copies, col_copies):
    f32 = jnp.float32
    rows, width = code_proj.shape
    cols = text_group.shape[0]
    lanes = math.gcd(cols // 2, 128)
    return pl.pallas_call(
        score_kernel,
        out_shape=(
            jax.ShapeDtypeStruct((cols, width), jnp.bfloat16),
            jax.ShapeDtypeStruct((rows, cols), f32),
            jax.ShapeDtypeStruct((row_copies, rows // lanes, lanes), f32),
            jax.ShapeDtypeStruct((col_copies, cols // lanes, lanes), f32),
        ),
        compiler_params=pltpu.CompilerParams(vmem_limit_bytes=40 << 20),
    )(text_group, weight, code_proj)


def mix_kernel(place_ref, exps_ref, row_ref, col_ref, back_ref, mixing_ref, sum_ref):
    lanes = row_ref.shape[2]
    here = place_ref[2]
    row_scale = 0.5 / jnp.sum(row_ref[...], axis=0)
    col_scale = 0.5 / jnp.sum(col_ref[...], axis=0)
    shape = (lanes, lanes)
    apart = lax.broadcasted_iota(jnp.int32, shape, 0) - lax.broadcasted_iota(jnp.int32, shape, 1)
    down = lax.broadcasted_iota(jnp.int32, shape, 0)
    for i in range(row_ref.shape[1]):
        rows = slice(i * lanes, (i + 1) * lanes)
        by_row = jnp.broadcast_to(row_scale[i : i + 1, :], shape).T
        first = down + (i * lanes - place_ref[0])
        inside = (first >= 0) & (first < here)
        for j in range(col_ref.shape[1]):
            cols = slice(j * lanes, (j + 1) * lanes)
            part = exps_ref[rows, cols] * (by_row + col_scale[j : j + 1, :])
            paired = inside & (apart == place_ref[0] - place_ref[1] + (j - i) * lanes)
            mixing_ref[rows, cols] = (part - jnp.where(paired, 1.0, 0.0)).astype(jnp.bfloat16)
    total = lax.dot_general(
        mixing_ref[...], back_ref[...], (((0,), (0,)), ((), ())), preferred_element_type=jnp.float32
    )
    sum_ref[...] = total.astype(jnp.bfloat16)


def mix(place, exps, row_parts, col_parts, code_back):
    rows, cols = exps.shape
    vmem = pl.BlockSpec(memory_space=pltpu.VMEM)
    return pl.pallas_call(
        mix_kernel,
        out_shape=(
            jax.ShapeDtypeStruct((rows, cols), jnp.bfloat16),
            jax.ShapeDtypeStruct((cols, code_back.shape[1]), jnp.bfloat16),
        ),
        in_specs=[pl.BlockSpec(memory_space=pltpu.SMEM), vmem, vmem, vmem, vmem],
        out_specs=(vmem, vmem),
        compiler_params=pltpu.CompilerParams(vmem_limit_bytes=40 << 20),
    )(place, exps, row_parts, col_parts, code_back)


def swap(block, name):
    return lax.ppermute(block, name, [(0, 1), (1, 0)])


def code_sum_kernel(core_ref, mixing_ref, text_ref, weight_ref, mine_ref, theirs_ref, back_ref, rows_ref):
    nt = (((1,), (1,)), ((), ()))
    step = text_ref.shape[0] // 2
    for i in range(2):
        part = text_ref[i * step : (i + 1) * step, :]
        back = lax.dot_general(part, weight_ref[...], nt, preferred_element_type=jnp.float32)
        back_ref[i * step : (i + 1) * step, :] = back.astype(jnp.bfloat16)
    chunk = 32
    for core, out_ref in ((1 - core_ref[0], theirs_ref), (core_ref[0], mine_ref)):
        for i in range(out_ref.shape[0] // chunk):
            start = pl.multiple_of(core * chunk + 2 * i * chunk, chunk)
            rows_ref[i * chunk : (i + 1) * chunk, :] = mixing_ref[pl.ds(start, chunk), :]
        total = jnp.dot(rows_ref[...], back_ref[...], preferred_element_type=jnp.float32)
        out_ref[...] = total.astype(out_ref.dtype)


def code_sum(core, mixing, text_proj, weight):
    rows, cols = mixing.shape
    depth = weight.shape[0]
    vmem = pl.BlockSpec(memory_space=pltpu.VMEM)
    half = jax.ShapeDtypeStruct((rows // 2, depth), jnp.bfloat16)
    return pl.pallas_call(
        code_sum_kernel,
        out_shape=(half, half),
        in_specs=[pl.BlockSpec(memory_space=pltpu.SMEM), vmem, vmem, vmem],
        out_specs=(vmem, vmem),
        scratch_shapes=[
            pltpu.VMEM((cols, depth), jnp.bfloat16),
            pltpu.VMEM((rows // 2, cols), jnp.bfloat16),
        ],
        compiler_params=pltpu.CompilerParams(vmem_limit_bytes=32 << 20),
        cost_estimate=pl.CostEstimate(flops=1 << 28, bytes_accessed=1 << 20, transcendentals=0),
    )(core.reshape(1), mixing, text_proj, weight)


def shards(code_tokens, text_tokens, code_weight, text_weight):
    f32, bf16 = jnp.float32, jnp.bfloat16
    nt = (((1,), (1,)), ((), ()))
    here, _, depth = code_tokens.shape
    core, side = lax.axis_index("c"), lax.axis_index("yl")
    code_row = lax.axis_index(CODE) * here
    text_row = lax.axis_index(TEXT) * here

    code_rows, text_rows = pool(code_tokens, text_tokens, lax.axis_size(TEXT))
    code_pair = lax.all_gather(code_rows, "zl", axis=0, tiled=True)
    code_pair, text_rows = lax.optimization_barrier((code_pair, text_rows))
    text_group = exchange(text_rows, TEXT).reshape(-1, depth)
    code_group = lax.all_gather(code_pair, CODE[:3], axis=0, tiled=True)

    code_proj = jnp.dot(code_group, code_weight, preferred_element_type=f32).astype(bf16)
    code_back = lax.dot_general(code_proj, text_weight, nt, preferred_element_type=f32).astype(bf16)
    code_back, text_group = lax.optimization_barrier((code_back, text_group))
    text_proj, exps, row_parts, col_parts = score_blocks(
        text_group, text_weight, code_proj, lax.axis_size(ROWS), lax.axis_size(TEXT)
    )
    live = (exps, code_proj, code_back, text_proj, code_row, text_row, core, side)
    row_parts, col_parts, *live = lax.optimization_barrier((exchange(row_parts, ROWS), col_parts, *live))
    row_parts, col_parts, *live = lax.optimization_barrier((row_parts, exchange(col_parts, TEXT), *live))
    exps, code_proj, code_back, text_proj, code_row, text_row, core, side = live
    row_total = jnp.sum(row_parts, axis=0).reshape(-1)
    col_total = jnp.sum(col_parts, axis=0).reshape(-1)

    own_code = lax.dynamic_slice_in_dim(code_proj, code_row, here).astype(f32)
    own_text = lax.dynamic_slice_in_dim(text_proj, text_row, here).astype(f32)
    own_scores = jnp.sum(own_code * own_text, axis=1) * score_scale
    own_row_total = lax.dynamic_slice_in_dim(row_total, code_row, here)
    own_col_total = lax.dynamic_slice_in_dim(col_total, text_row, here)
    pair_loss = 0.5 * (jnp.log(own_row_total) + jnp.log(own_col_total)) - own_scores

    place = jnp.stack([code_row, text_row, jnp.int32(here)])
    mixing, text_parts = mix(place, exps, row_parts, col_parts, code_back)
    text_proj, text_parts = lax.optimization_barrier((text_proj, text_parts))
    text_parts = exchange(text_parts.reshape(-1, here, depth), TEXT)

    mine, theirs = code_sum(core, mixing, text_proj, code_weight)
    code_parts = (mine.astype(f32) + swap(theirs, "c").astype(f32)).astype(bf16)
    code_parts = code_parts.reshape(-1, 2, 2 * here, depth)
    mine = lax.dynamic_index_in_dim(code_parts, side, 1, keepdims=False)
    theirs = lax.dynamic_index_in_dim(code_parts, 1 - side, 1, keepdims=False)
    code_parts = (mine.astype(f32) + swap(theirs, "yl").astype(f32)).astype(bf16)
    code_parts, text_parts = lax.optimization_barrier((code_parts, text_parts))
    code_parts = exchange(code_parts.reshape(-1, here, depth), ("yh", "zl"))
    grad_code = score_scale * jnp.sum(code_parts.astype(f32), axis=0)
    grad_text = score_scale * jnp.sum(text_parts.astype(f32), axis=0)
    return pair_loss, grad_code.astype(bf16), grad_text.astype(bf16)


def solution(mesh):
    n_outer, n_inner = mesh.shape["outer"], mesh.shape["inner"]
    side = math.isqrt(n_inner)
    sizes = (n_outer // 2, 2, side // 2, 2, side // 2, 2)
    fine = Mesh(mesh.devices.reshape(sizes), ("x", "c", "zh", "zl", "yh", "yl"))
    every = P(fine.axis_names)
    return jax.shard_map(
        shards,
        mesh=fine,
        in_specs=(every, every, P(), P()),
        out_specs=(every, every, every),
        check_vma=False,
    )
```

```python
import math

import jax
import jax.numpy as jnp
from jax import lax
from jax.experimental import pallas as pl
from jax.experimental.pallas import tpu as pltpu
from jax.sharding import Mesh
from jax.sharding import PartitionSpec as P

score_scale = 0.1
CODE = ("yh", "yl", "c", "zl")
ROWS = ("c", "zl", "yh", "yl")
TEXT = ("x", "zh")


def pool_kernel(code_ref, text_ref, code_out, text_out):
    for tokens, out in ((code_ref, code_out), (text_ref, text_out)):
        total = jnp.sum(tokens[...].astype(jnp.float32), axis=1)
        rows = (total * (1.0 / tokens.shape[1])).astype(jnp.bfloat16)
        out[...] = rows if out is code_out else jnp.broadcast_to(rows[None], out.shape)


def pool(code_tokens, text_tokens, copies):
    here, _, depth = code_tokens.shape
    return pl.pallas_call(
        pool_kernel,
        out_shape=(
            jax.ShapeDtypeStruct((here, depth), jnp.bfloat16),
            jax.ShapeDtypeStruct((copies, here, depth), jnp.bfloat16),
        ),
    )(code_tokens, text_tokens)


def exchange(parts, axes):
    return lax.all_to_all(parts, axes, split_axis=0, concat_axis=0, tiled=True)


def fan_out(block, axes):
    members = lax.axis_size(axes)
    spread = jnp.broadcast_to(block[None], (members,) + block.shape)
    return exchange(lax.optimization_barrier(spread), axes)


def score_kernel(
    text_ref, weight_ref, code_ref, proj_out, exps_out, row_ref, col_ref, proj_ref, exps_ref, sems
):
    nt = (((1,), (1,)), ((), ()))
    lanes = row_ref.shape[2]
    step = text_ref.shape[0] // 2
    copies = []
    row_sum = jnp.zeros((code_ref.shape[0], lanes), jnp.float32)
    for i in range(2):
        part = jnp.dot(
            text_ref[i * step : (i + 1) * step, :], weight_ref[...], preferred_element_type=jnp.float32
        ).astype(jnp.bfloat16)
        proj_ref[i * step : (i + 1) * step, :] = part
        scores = lax.dot_general(code_ref[...], part, nt, preferred_element_type=jnp.float32)
        exps = jnp.exp(scores * score_scale)
        exps_ref[:, i * step : (i + 1) * step] = exps
        half = pl.ds(i * step, step)
        copies += [
            pltpu.make_async_copy(proj_ref.at[half, :], proj_out.at[half, :], sems.at[2 * i]),
            pltpu.make_async_copy(exps_ref.at[:, half], exps_out.at[:, half], sems.at[2 * i + 1]),
        ]
        copies[-2].start()
        copies[-1].start()
        col_sum = jnp.sum(exps, axis=0, keepdims=True)
        for j in range(step // lanes):
            row_sum += exps[:, j * lanes : (j + 1) * lanes]
            at = i * (step // lanes) + j
            total = jnp.broadcast_to(col_sum[:, j * lanes : (j + 1) * lanes], (col_ref.shape[0], lanes))
            col_ref[:, at, :] = total
    row_sum = jnp.sum(row_sum.T, axis=0, keepdims=True)
    for j in range(row_ref.shape[1]):
        total = jnp.broadcast_to(row_sum[:, j * lanes : (j + 1) * lanes], (row_ref.shape[0], lanes))
        row_ref[:, j, :] = total
    for copy in copies:
        copy.wait()


def score_blocks(text_group, weight, code_proj, row_copies, col_copies):
    f32 = jnp.float32
    rows, width = code_proj.shape
    cols = text_group.shape[0]
    lanes = math.gcd(cols // 2, 128)
    return pl.pallas_call(
        score_kernel,
        out_shape=(
            pltpu.HBM((cols, width), jnp.bfloat16),
            pltpu.HBM((rows, cols), f32),
            jax.ShapeDtypeStruct((row_copies, rows // lanes, lanes), f32),
            jax.ShapeDtypeStruct((col_copies, cols // lanes, lanes), f32),
        ),
        out_specs=(
            pl.BlockSpec(memory_space=pltpu.HBM),
            pl.BlockSpec(memory_space=pltpu.HBM),
            pl.BlockSpec(memory_space=pltpu.VMEM),
            pl.BlockSpec(memory_space=pltpu.VMEM),
        ),
        scratch_shapes=[
            pltpu.VMEM((cols, width), jnp.bfloat16),
            pltpu.VMEM((rows, cols), f32),
            pltpu.SemaphoreType.DMA((4,)),
        ],
        compiler_params=pltpu.CompilerParams(vmem_limit_bytes=40 << 20),
    )(text_group, weight, code_proj)


def in_hbm(array):
    return pltpu.with_memory_space_constraint(array, pltpu.HBM)


def mix_kernel(
    place_ref, exps_in, row_ref, col_ref, back_in, mixing_ref, sum_ref, exps_ref, back_ref, sems
):
    lanes = row_ref.shape[2]
    here = place_ref[2]
    fetch_exps = pltpu.make_async_copy(exps_in, exps_ref, sems.at[0])
    fetch_back = pltpu.make_async_copy(back_in, back_ref, sems.at[1])
    fetch_exps.start()
    fetch_back.start()
    row_scale = 0.5 / jnp.sum(row_ref[...], axis=0)
    col_scale = 0.5 / jnp.sum(col_ref[...], axis=0)
    shape = (lanes, lanes)
    apart = lax.broadcasted_iota(jnp.int32, shape, 0) - lax.broadcasted_iota(jnp.int32, shape, 1)
    down = lax.broadcasted_iota(jnp.int32, shape, 0)
    fetch_exps.wait()
    for i in range(row_ref.shape[1]):
        rows = slice(i * lanes, (i + 1) * lanes)
        by_row = jnp.broadcast_to(row_scale[i : i + 1, :], shape).T
        first = down + (i * lanes - place_ref[0])
        inside = (first >= 0) & (first < here)
        for j in range(col_ref.shape[1]):
            cols = slice(j * lanes, (j + 1) * lanes)
            part = exps_ref[rows, cols] * (by_row + col_scale[j : j + 1, :])
            paired = inside & (apart == place_ref[0] - place_ref[1] + (j - i) * lanes)
            mixing_ref[rows, cols] = (part - jnp.where(paired, 1.0, 0.0)).astype(jnp.bfloat16)
    fetch_back.wait()
    total = lax.dot_general(
        mixing_ref[...], back_ref[...], (((0,), (0,)), ((), ())), preferred_element_type=jnp.float32
    )
    sum_ref[...] = total.astype(jnp.bfloat16)


def mix(place, exps, row_parts, col_parts, code_back):
    rows, cols = exps.shape
    vmem, hbm = pl.BlockSpec(memory_space=pltpu.VMEM), pl.BlockSpec(memory_space=pltpu.HBM)
    return pl.pallas_call(
        mix_kernel,
        out_shape=(
            jax.ShapeDtypeStruct((rows, cols), jnp.bfloat16),
            jax.ShapeDtypeStruct((cols, code_back.shape[1]), jnp.bfloat16),
        ),
        in_specs=[pl.BlockSpec(memory_space=pltpu.SMEM), hbm, vmem, vmem, hbm],
        out_specs=(pl.BlockSpec(), pl.BlockSpec()),
        scratch_shapes=[
            pltpu.VMEM(exps.shape, exps.dtype),
            pltpu.VMEM(code_back.shape, code_back.dtype),
            pltpu.SemaphoreType.DMA((2,)),
        ],
        compiler_params=pltpu.CompilerParams(vmem_limit_bytes=40 << 20),
    )(place, in_hbm(exps), row_parts, col_parts, in_hbm(code_back))


def swap(block, name):
    return lax.ppermute(block, name, [(0, 1), (1, 0)])


def code_sum_kernel(core_ref, mixing_ref, text_ref, weight_ref, mine_ref, theirs_ref, back_ref, rows_ref):
    nt = (((1,), (1,)), ((), ()))
    step = text_ref.shape[0] // 2
    for i in range(2):
        part = text_ref[i * step : (i + 1) * step, :]
        back = lax.dot_general(part, weight_ref[...], nt, preferred_element_type=jnp.float32)
        back_ref[i * step : (i + 1) * step, :] = back.astype(jnp.bfloat16)
    chunk = 32
    for core, out_ref in ((1 - core_ref[0], theirs_ref), (core_ref[0], mine_ref)):
        for i in range(out_ref.shape[0] // chunk):
            start = pl.multiple_of(core * chunk + 2 * i * chunk, chunk)
            rows_ref[i * chunk : (i + 1) * chunk, :] = mixing_ref[pl.ds(start, chunk), :]
        total = jnp.dot(rows_ref[...], back_ref[...], preferred_element_type=jnp.float32)
        out_ref[...] = total.astype(out_ref.dtype)


def code_sum(core, mixing, text_proj, weight):
    rows, cols = mixing.shape
    depth = weight.shape[0]
    whole = pl.BlockSpec()
    half = jax.ShapeDtypeStruct((rows // 2, depth), jnp.bfloat16)
    return pl.pallas_call(
        code_sum_kernel,
        out_shape=(half, half),
        in_specs=[pl.BlockSpec(memory_space=pltpu.SMEM), whole, whole, whole],
        out_specs=(whole, whole),
        scratch_shapes=[
            pltpu.VMEM((cols, depth), jnp.bfloat16),
            pltpu.VMEM((rows // 2, cols), jnp.bfloat16),
        ],
        compiler_params=pltpu.CompilerParams(vmem_limit_bytes=32 << 20),
        cost_estimate=pl.CostEstimate(flops=1 << 28, bytes_accessed=1 << 20, transcendentals=0),
    )(core.reshape(1), mixing, text_proj, weight)


def shards(code_tokens, text_tokens, code_weight, text_weight):
    f32, bf16 = jnp.float32, jnp.bfloat16
    nt = (((1,), (1,)), ((), ()))
    here, _, depth = code_tokens.shape
    core, side = lax.axis_index("c"), lax.axis_index("yl")
    code_row = lax.axis_index(CODE) * here
    text_row = lax.axis_index(TEXT) * here

    code_rows, text_rows = pool(code_tokens, text_tokens, lax.axis_size(TEXT))
    code_pair = lax.all_gather(code_rows, "zl", axis=0, tiled=True)
    code_pair, text_rows = lax.optimization_barrier((code_pair, text_rows))
    text_group = exchange(text_rows, TEXT).reshape(-1, depth)
    code_group = lax.all_gather(code_pair, CODE[:3], axis=0, tiled=True)

    code_proj = jnp.dot(code_group, code_weight, preferred_element_type=f32).astype(bf16)
    code_back = lax.dot_general(code_proj, text_weight, nt, preferred_element_type=f32).astype(bf16)
    code_back, text_group = lax.optimization_barrier((code_back, text_group))
    text_proj, exps, row_parts, col_parts = score_blocks(
        text_group, text_weight, code_proj, lax.axis_size(ROWS), lax.axis_size(TEXT)
    )
    live = (exps, code_proj, code_back, text_proj, code_row, text_row, core, side)
    row_parts, col_parts, *live = lax.optimization_barrier((exchange(row_parts, ROWS), col_parts, *live))
    row_parts, col_parts, *live = lax.optimization_barrier((row_parts, exchange(col_parts, TEXT), *live))
    exps, code_proj, code_back, text_proj, code_row, text_row, core, side = live
    row_total = jnp.sum(row_parts, axis=0).reshape(-1)
    col_total = jnp.sum(col_parts, axis=0).reshape(-1)

    own_code = lax.dynamic_slice_in_dim(code_proj, code_row, here).astype(f32)
    own_text = lax.dynamic_slice_in_dim(text_proj, text_row, here).astype(f32)
    own_scores = jnp.sum(own_code * own_text, axis=1) * score_scale
    own_row_total = lax.dynamic_slice_in_dim(row_total, code_row, here)
    own_col_total = lax.dynamic_slice_in_dim(col_total, text_row, here)
    pair_loss = 0.5 * (jnp.log(own_row_total) + jnp.log(own_col_total)) - own_scores

    place = jnp.stack([code_row, text_row, jnp.int32(here)])
    mixing, text_parts = mix(place, exps, row_parts, col_parts, code_back)
    text_proj, text_parts = lax.optimization_barrier((text_proj, text_parts))
    text_parts = exchange(text_parts.reshape(-1, here, depth), TEXT)

    mine, theirs = code_sum(core, mixing, text_proj, code_weight)
    code_parts = (mine.astype(f32) + swap(theirs, "c").astype(f32)).astype(bf16)
    code_parts = code_parts.reshape(-1, 2, 2 * here, depth)
    mine = lax.dynamic_index_in_dim(code_parts, side, 1, keepdims=False)
    theirs = lax.dynamic_index_in_dim(code_parts, 1 - side, 1, keepdims=False)
    code_parts = (mine.astype(f32) + swap(theirs, "yl").astype(f32)).astype(bf16)
    code_parts, text_parts = lax.optimization_barrier((code_parts, text_parts))
    code_parts = exchange(code_parts.reshape(-1, here, depth), ("yh", "zl"))
    grad_code = score_scale * jnp.sum(code_parts.astype(f32), axis=0)
    grad_text = score_scale * jnp.sum(text_parts.astype(f32), axis=0)
    return pair_loss, grad_code.astype(bf16), grad_text.astype(bf16)


def solution(mesh):
    n_outer, n_inner = mesh.shape["outer"], mesh.shape["inner"]
    side = math.isqrt(n_inner)
    sizes = (n_outer // 2, 2, side // 2, 2, side // 2, 2)
    fine = Mesh(mesh.devices.reshape(sizes), ("x", "c", "zh", "zl", "yh", "yl"))
    every = P(fine.axis_names)
    return jax.shard_map(
        shards,
        mesh=fine,
        in_specs=(every, every, P(), P()),
        out_specs=(every, every, every),
        check_vma=False,
    )
```

```python
import math

import jax
import jax.numpy as jnp
from jax import lax
from jax.experimental import pallas as pl
from jax.experimental.pallas import tpu as pltpu
from jax.sharding import Mesh
from jax.sharding import PartitionSpec as P

score_scale = 0.1
CODE = ("yh", "yl", "c", "zl")
ROWS = ("c", "zl", "yh", "yl")
TEXT = ("x", "zh")


def pool_kernel(code_ref, text_ref, code_out, text_out):
    for tokens, out in ((code_ref, code_out), (text_ref, text_out)):
        total = jnp.sum(tokens[...].astype(jnp.float32), axis=1)
        rows = (total * (1.0 / tokens.shape[1])).astype(jnp.bfloat16)
        out[...] = rows if out is code_out else jnp.broadcast_to(rows[None], out.shape)


def pool(code_tokens, text_tokens, copies):
    here, _, depth = code_tokens.shape
    return pl.pallas_call(
        pool_kernel,
        out_shape=(
            jax.ShapeDtypeStruct((here, depth), jnp.bfloat16),
            jax.ShapeDtypeStruct((copies, here, depth), jnp.bfloat16),
        ),
    )(code_tokens, text_tokens)


def exchange(parts, axes):
    return lax.all_to_all(parts, axes, split_axis=0, concat_axis=0, tiled=True)


def fan_out(block, axes):
    members = lax.axis_size(axes)
    spread = jnp.broadcast_to(block[None], (members,) + block.shape)
    return exchange(lax.optimization_barrier(spread), axes)


def score_kernel(
    text_ref, weight_ref, code_ref, proj_out, exps_out, row_ref, col_ref, proj_ref, exps_ref, sems
):
    nt = (((1,), (1,)), ((), ()))
    lanes = row_ref.shape[2]
    step = text_ref.shape[0] // 2
    copies = []
    row_sum = jnp.zeros((code_ref.shape[0], lanes), jnp.float32)
    for i in range(2):
        part = jnp.dot(
            text_ref[i * step : (i + 1) * step, :], weight_ref[...], preferred_element_type=jnp.float32
        ).astype(jnp.bfloat16)
        proj_ref[i * step : (i + 1) * step, :] = part
        scores = lax.dot_general(code_ref[...], part, nt, preferred_element_type=jnp.float32)
        exps = jnp.exp(scores * score_scale)
        exps_ref[:, i * step : (i + 1) * step] = exps
        half = pl.ds(i * step, step)
        copies += [
            pltpu.make_async_copy(proj_ref.at[half, :], proj_out.at[half, :], sems.at[2 * i]),
            pltpu.make_async_copy(exps_ref.at[:, half], exps_out.at[:, half], sems.at[2 * i + 1]),
        ]
        copies[-2].start()
        copies[-1].start()
        col_sum = jnp.sum(exps, axis=0, keepdims=True)
        for j in range(step // lanes):
            row_sum += exps[:, j * lanes : (j + 1) * lanes]
            at = i * (step // lanes) + j
            total = jnp.broadcast_to(col_sum[:, j * lanes : (j + 1) * lanes], (col_ref.shape[0], lanes))
            col_ref[:, at, :] = total
    row_sum = jnp.sum(row_sum.T, axis=0, keepdims=True)
    for j in range(row_ref.shape[1]):
        total = jnp.broadcast_to(row_sum[:, j * lanes : (j + 1) * lanes], (row_ref.shape[0], lanes))
        row_ref[:, j, :] = total
    for copy in copies:
        copy.wait()


def score_blocks(text_group, weight, code_proj, row_copies, col_copies):
    f32 = jnp.float32
    rows, width = code_proj.shape
    cols = text_group.shape[0]
    lanes = math.gcd(cols // 2, 128)
    return pl.pallas_call(
        score_kernel,
        out_shape=(
            pltpu.HBM((cols, width), jnp.bfloat16),
            pltpu.HBM((rows, cols), f32),
            jax.ShapeDtypeStruct((row_copies, rows // lanes, lanes), f32),
            jax.ShapeDtypeStruct((col_copies, cols // lanes, lanes), f32),
        ),
        out_specs=(
            pl.BlockSpec(memory_space=pltpu.HBM),
            pl.BlockSpec(memory_space=pltpu.HBM),
            pl.BlockSpec(memory_space=pltpu.VMEM),
            pl.BlockSpec(memory_space=pltpu.VMEM),
        ),
        scratch_shapes=[
            pltpu.VMEM((cols, width), jnp.bfloat16),
            pltpu.VMEM((rows, cols), f32),
            pltpu.SemaphoreType.DMA((4,)),
        ],
        compiler_params=pltpu.CompilerParams(vmem_limit_bytes=40 << 20),
    )(text_group, weight, code_proj)


def in_hbm(array):
    return pltpu.with_memory_space_constraint(array, pltpu.HBM)


def mix_kernel(
    place_ref, exps_in, row_ref, col_ref, back_in, mixing_ref, sum_ref, exps_ref, back_ref, sems
):
    lanes = row_ref.shape[2]
    here = place_ref[2]
    fetch_exps = pltpu.make_async_copy(exps_in, exps_ref, sems.at[0])
    fetch_back = pltpu.make_async_copy(back_in, back_ref, sems.at[1])
    fetch_exps.start()
    fetch_back.start()
    row_scale = 0.5 / jnp.sum(row_ref[...], axis=0)
    col_scale = 0.5 / jnp.sum(col_ref[...], axis=0)
    shape = (lanes, lanes)
    apart = lax.broadcasted_iota(jnp.int32, shape, 0) - lax.broadcasted_iota(jnp.int32, shape, 1)
    down = lax.broadcasted_iota(jnp.int32, shape, 0)
    fetch_exps.wait()
    for i in range(row_ref.shape[1]):
        rows = slice(i * lanes, (i + 1) * lanes)
        by_row = jnp.broadcast_to(row_scale[i : i + 1, :], shape).T
        first = down + (i * lanes - place_ref[0])
        inside = (first >= 0) & (first < here)
        for j in range(col_ref.shape[1]):
            cols = slice(j * lanes, (j + 1) * lanes)
            part = exps_ref[rows, cols] * (by_row + col_scale[j : j + 1, :])
            paired = inside & (apart == place_ref[0] - place_ref[1] + (j - i) * lanes)
            mixing_ref[rows, cols] = (part - jnp.where(paired, 1.0, 0.0)).astype(jnp.bfloat16)
    fetch_back.wait()
    total = lax.dot_general(
        mixing_ref[...], back_ref[...], (((0,), (0,)), ((), ())), preferred_element_type=jnp.float32
    )
    sum_ref[...] = total.astype(jnp.bfloat16)


def mix(place, exps, row_parts, col_parts, code_back):
    rows, cols = exps.shape
    vmem, hbm = pl.BlockSpec(memory_space=pltpu.VMEM), pl.BlockSpec(memory_space=pltpu.HBM)
    return pl.pallas_call(
        mix_kernel,
        out_shape=(
            jax.ShapeDtypeStruct((rows, cols), jnp.bfloat16),
            jax.ShapeDtypeStruct((cols, code_back.shape[1]), jnp.bfloat16),
        ),
        in_specs=[pl.BlockSpec(memory_space=pltpu.SMEM), hbm, vmem, vmem, hbm],
        out_specs=(pl.BlockSpec(), pl.BlockSpec()),
        scratch_shapes=[
            pltpu.VMEM(exps.shape, exps.dtype),
            pltpu.VMEM(code_back.shape, code_back.dtype),
            pltpu.SemaphoreType.DMA((2,)),
        ],
        compiler_params=pltpu.CompilerParams(vmem_limit_bytes=40 << 20),
    )(place, in_hbm(exps), row_parts, col_parts, in_hbm(code_back))


def swap(block, name):
    return lax.ppermute(block, name, [(0, 1), (1, 0)])


def code_sum_kernel(core_ref, mixing_ref, text_ref, weight_ref, mine_ref, theirs_ref, back_ref, rows_ref):
    nt = (((1,), (1,)), ((), ()))
    step = text_ref.shape[0] // 2
    for i in range(2):
        part = text_ref[i * step : (i + 1) * step, :]
        back = lax.dot_general(part, weight_ref[...], nt, preferred_element_type=jnp.float32)
        back_ref[i * step : (i + 1) * step, :] = back.astype(jnp.bfloat16)
    chunk = 32
    for core, out_ref in ((1 - core_ref[0], theirs_ref), (core_ref[0], mine_ref)):
        for i in range(out_ref.shape[0] // chunk):
            start = pl.multiple_of(core * chunk + 2 * i * chunk, chunk)
            rows_ref[i * chunk : (i + 1) * chunk, :] = mixing_ref[pl.ds(start, chunk), :]
        total = jnp.dot(rows_ref[...], back_ref[...], preferred_element_type=jnp.float32)
        out_ref[...] = total.astype(out_ref.dtype)


def code_sum(core, mixing, text_proj, weight):
    rows, cols = mixing.shape
    depth = weight.shape[0]
    whole = pl.BlockSpec()
    half = jax.ShapeDtypeStruct((rows // 2, depth), jnp.bfloat16)
    return pl.pallas_call(
        code_sum_kernel,
        out_shape=(half, half),
        in_specs=[pl.BlockSpec(memory_space=pltpu.SMEM), whole, whole, whole],
        out_specs=(whole, whole),
        scratch_shapes=[
            pltpu.VMEM((cols, depth), jnp.bfloat16),
            pltpu.VMEM((rows // 2, cols), jnp.bfloat16),
        ],
        compiler_params=pltpu.CompilerParams(vmem_limit_bytes=32 << 20),
        cost_estimate=pl.CostEstimate(flops=1 << 28, bytes_accessed=1 << 20, transcendentals=0),
    )(core.reshape(1), mixing, text_proj, weight)


def shards(code_tokens, text_tokens, code_weight, text_weight):
    f32, bf16 = jnp.float32, jnp.bfloat16
    nt = (((1,), (1,)), ((), ()))
    here, _, depth = code_tokens.shape
    core, side = lax.axis_index("c"), lax.axis_index("yl")
    code_row = lax.axis_index(CODE) * here
    text_row = lax.axis_index(TEXT) * here

    code_rows, text_rows = pool(code_tokens, text_tokens, lax.axis_size(TEXT))
    code_pair = lax.all_gather(code_rows, "zl", axis=0, tiled=True)
    code_pair, text_rows = lax.optimization_barrier((code_pair, text_rows))
    text_group = exchange(text_rows, TEXT).reshape(-1, depth)
    code_group = lax.all_gather(code_pair, CODE[:3], axis=0, tiled=True)

    code_proj = jnp.dot(code_group, code_weight, preferred_element_type=f32).astype(bf16)
    code_back = lax.dot_general(code_proj, text_weight, nt, preferred_element_type=f32).astype(bf16)
    code_back, text_group = lax.optimization_barrier((code_back, text_group))
    text_proj, exps, row_parts, col_parts = score_blocks(
        text_group, text_weight, code_proj, lax.axis_size(ROWS), 1
    )
    live = (exps, code_proj, code_back, text_proj, code_row, text_row, core, side)
    row_parts = exchange(row_parts, ROWS)
    col_part = lax.psum(col_parts[0], "zh")
    row_parts, col_part, *live = lax.optimization_barrier((row_parts, col_part, *live))
    col_parts = fan_out(col_part, "x")
    row_parts, col_parts, *live = lax.optimization_barrier((row_parts, col_parts, *live))
    exps, code_proj, code_back, text_proj, code_row, text_row, core, side = live
    row_total = jnp.sum(row_parts, axis=0).reshape(-1)
    col_total = jnp.sum(col_parts, axis=0).reshape(-1)

    own_code = lax.dynamic_slice_in_dim(code_proj, code_row, here).astype(f32)
    own_text = lax.dynamic_slice_in_dim(text_proj, text_row, here).astype(f32)
    own_scores = jnp.sum(own_code * own_text, axis=1) * score_scale
    own_row_total = lax.dynamic_slice_in_dim(row_total, code_row, here)
    own_col_total = lax.dynamic_slice_in_dim(col_total, text_row, here)
    pair_loss = 0.5 * (jnp.log(own_row_total) + jnp.log(own_col_total)) - own_scores

    place = jnp.stack([code_row, text_row, jnp.int32(here)])
    mixing, text_parts = mix(place, exps, row_parts, col_parts, code_back)
    text_proj, text_parts = lax.optimization_barrier((text_proj, text_parts))
    text_parts = exchange(text_parts.reshape(-1, here, depth), TEXT)

    mine, theirs = code_sum(core, mixing, text_proj, code_weight)
    code_parts = (mine.astype(f32) + swap(theirs, "c").astype(f32)).astype(bf16)
    code_parts = code_parts.reshape(-1, 2, 2 * here, depth)
    mine = lax.dynamic_index_in_dim(code_parts, side, 1, keepdims=False)
    theirs = lax.dynamic_index_in_dim(code_parts, 1 - side, 1, keepdims=False)
    code_parts = (mine.astype(f32) + swap(theirs, "yl").astype(f32)).astype(bf16)
    code_parts, text_parts = lax.optimization_barrier((code_parts, text_parts))
    code_parts = exchange(code_parts.reshape(-1, here, depth), ("yh", "zl"))
    grad_code = score_scale * jnp.sum(code_parts.astype(f32), axis=0)
    grad_text = score_scale * jnp.sum(text_parts.astype(f32), axis=0)
    return pair_loss, grad_code.astype(bf16), grad_text.astype(bf16)


def solution(mesh):
    n_outer, n_inner = mesh.shape["outer"], mesh.shape["inner"]
    side = math.isqrt(n_inner)
    sizes = (n_outer // 2, 2, side // 2, 2, side // 2, 2)
    fine = Mesh(mesh.devices.reshape(sizes), ("x", "c", "zh", "zl", "yh", "yl"))
    every = P(fine.axis_names)
    return jax.shard_map(
        shards,
        mesh=fine,
        in_specs=(every, every, P(), P()),
        out_specs=(every, every, every),
        check_vma=False,
    )
```
